512 devices in a mesh: tok: 8 (over z_hi, x), blk: 64 (over z_lo, y, core).
Axes of the slice: x: 4, y: 8, z: 8 (z_hi: 2, z_lo: 4; z = z_hi * 4 + z_lo), core: 2. Of those that a mesh axis runs over, the one named last changes fastest.
Arguments:
- grad_out: bfloat16 [8192, 8192], P('tok', 'blk'), may hold values from -6 to 6
- acts: bfloat16 [8192, 8192], P('tok', 'blk'), may hold values from -6 to 6
- stat_old: float32 [8, 64, 512, 512], P('tok', 'blk'), may hold values from -1 to 6, as said below
- root_old: float32 [8, 64, 512, 512], P('tok', 'blk'), may hold values from -1 to 2, as said below
- assign: int32 [64, 8], P('blk'), may hold values from 0 to 7, as said below
Outputs:
- roots: float32 [8, 64, 512, 512], P('tok', 'blk')
- precond: float32 [8, 64, 256, 512], P('tok', 'blk')
The draws below stay inside these ranges and needn't reach their ends.
Inputs may be any that keep to these rules, and one draw needn't show every extreme that they name: `assign`: row j gives each of its 8 slots a job 2 b + s with b < 4 and s in 0, 1; every job once in a row; slots 2 m and 2 m + 1 hold the two sides of one block. `stat_old`: each slot's matrix is symmetric and positive definite. `root_old`: each slot's matrix is symmetric.
All inputs are finite; a program needn't handle non-finite values.
Results may differ from the reference program's by a relative error of at most 0.0003.
Values may be sent and summed in bfloat16 or wider, within the bound.
A program may use at most 64 MiB of HBM per device.

```python
import math
import jax
import jax.numpy as jnp
from jax import lax

DM = 8192
BS = 512
TOK_DEV = 1024
ITERS = 2
STRIPS = 16
GROUP_BLOCKS = 4
COLS = 8192
TOKENS = 8192
N_TOK = 8
N_BLK = 64


def diagonal_scales(key):
    base = jax.random.fold_in(key, 11)
    logs = jax.random.uniform(base, (N_TOK, N_BLK, BS), jnp.float32, jnp.log(0.25), jnp.log(4.0))
    return jnp.exp(logs)


def older_scales(key):
    diagonal = diagonal_scales(key)
    base = jax.random.fold_in(key, 13)
    ageing = jax.random.uniform(base, (N_TOK, N_BLK, BS), jnp.float32, 1.0, 2.5)
    return diagonal * ageing


def symmetric_noise(key, salt):
    inner = jax.random.fold_in(key, salt)
    shape_full = (N_TOK, N_BLK, BS, BS)
    raw_noise = jax.random.normal(inner, shape_full, jnp.float32)
    identity = jnp.eye(BS, dtype=jnp.float32)
    return (raw_noise + jnp.swapaxes(raw_noise, -1, -2)) * 0.7071 * (1.0 - identity)


def draw_stat_old(key, part):
    diagonal = diagonal_scales(key)
    noise_part = symmetric_noise(key, 29)
    identity = jnp.eye(BS, dtype=jnp.float32)
    couple = jnp.sqrt(diagonal[..., :, None] * diagonal[..., None, :])
    return identity * diagonal[..., None] + 0.004 * couple * noise_part


def draw_root_old(key, part):
    diagonal = older_scales(key)
    noise_part = symmetric_noise(key, 37)
    identity = jnp.eye(BS, dtype=jnp.float32)
    couple = (diagonal[..., :, None] * diagonal[..., None, :]) ** (-0.125)
    return identity * (diagonal ** (-0.25))[..., None] + 0.002 * couple * noise_part


def draw_assign(key, part):
    pair_count = N_TOK // 2
    base = jax.random.fold_in(key, 23)
    order_keys = jax.random.split(jax.random.fold_in(base, 1), N_BLK)
    orders = jax.vmap(lambda inner: jax.random.permutation(inner, pair_count))(order_keys)
    flip_bits = jax.random.randint(jax.random.fold_in(base, 2), (N_BLK, pair_count), 0, 2)
    first_job = 2 * orders + flip_bits
    second_job = 2 * orders + 1 - flip_bits
    return jnp.stack([first_job, second_job], axis=-1).reshape(N_BLK, N_TOK).astype(jnp.int32)


def steps_of(key, dims, pieces, smallest, high):
    level, own = 1.0, jax.random.fold_in(key, 6)
    for axis_at, parts in pieces:
        heights = jnp.exp(jax.random.uniform(jax.random.fold_in(own, axis_at), (parts,), jnp.float32, smallest / len(pieces), high / len(pieces)))
        level = level * jnp.repeat(heights, dims[axis_at] // parts).reshape([-1 if axis == axis_at else 1 for axis in range(len(dims))])
    return level


def gaussian(stream_key, shape, scale, limit, pieces=(), held_as=jnp.bfloat16):
    array = scale * jax.random.normal(stream_key, shape, jnp.float32)
    if pieces:
        array = array * steps_of(stream_key, shape, pieces, -0.22, 0.18)
    return jnp.clip(array, -limit, limit).astype(held_as)


def setup_inputs(seed: int = 0) -> dict:
    splits = jax.random.split(jax.random.key(seed), 6)
    grad_out = gaussian(splits[0], (TOKENS, DM), 1.0, 6.0, ((0, 8), (1, 64)))
    acts = gaussian(splits[1], (TOKENS, COLS), 1.0, 6.0, ((0, 8), (1, 64)))
    stat_old = draw_stat_old(jax.random.fold_in(splits[5], 71), 0)
    root_old = draw_root_old(jax.random.fold_in(splits[5], 71), 0)
    assign = draw_assign(jax.random.fold_in(splits[5], 71), 0)
    return {"grad_out": grad_out, "acts": acts, "stat_old": stat_old, "root_old": root_old, "assign": assign}


BETA = 0.9
DAMPING = 0.001

def product(lhs_matrix, rhs_matrix):
    return jnp.dot(lhs_matrix, rhs_matrix, precision=lax.Precision.HIGHEST, preferred_element_type=jnp.float32)

def newton_root(statistic, warm_root, square):
    identity = jnp.eye(square.shape[0], dtype=jnp.float32)
    factor = BETA * statistic + (1.0 - BETA) * square + DAMPING * identity
    root_square = product(warm_root, warm_root)
    coupled = product(product(root_square, root_square), factor)
    current = warm_root
    for iteration in range(ITERS):
        update = (5.0 * identity - coupled) * 0.25
        current = product(current, update)
        if iteration + 1 < ITERS:
            update_square = product(update, update)
            coupled = product(product(update_square, update_square), coupled)
    return current

def reference(grad_out, acts, stat_old, root_old, assign):
    group_width = GROUP_BLOCKS * BS
    scaling = 1.0 / math.sqrt(TOKENS)
    shard_cols = DM // N_BLK
    strided = grad_out.reshape(TOKENS, N_BLK // STRIPS, STRIPS, shard_cols)

    def per_column(column):
        strip_index = (column % STRIPS).astype(jnp.int32)
        col_start = (column // STRIPS * group_width).astype(jnp.int32)
        rows_part = lax.dynamic_slice_in_dim(strided, strip_index, 1, 2).reshape(TOKENS, BS)
        rows_part = rows_part.astype(jnp.float32).reshape(N_TOK, TOK_DEV, BS)
        cols_part = lax.dynamic_slice_in_dim(acts, col_start, group_width, 1).astype(jnp.float32).reshape(N_TOK, TOK_DEV, group_width)
        partial_value = jnp.einsum('ktr,ktc->krc', rows_part, cols_part, precision=lax.Precision.HIGHEST) * scaling
        gradient = lax.optimization_barrier(jnp.sum(partial_value, axis=0))
        blocks = gradient.reshape(BS, GROUP_BLOCKS, BS).transpose(1, 0, 2)
        job_table = assign[column]

        def per_slot(position):
            job_index = job_table[position]
            chosen = blocks[job_index // 2]
            oriented = jnp.where(job_index % 2 == 0, chosen, chosen.T)
            square = product(oriented, oriented.T) / TOKENS
            return newton_root(stat_old[position, column], root_old[position, column], square)
        root_stack = lax.map(per_slot, jnp.arange(N_TOK, dtype=jnp.int32))

        def per_output(position):
            job_index = job_table[position]
            side_bit = job_index % 2
            chosen = blocks[job_index // 2]
            own_root = root_stack[position]
            other_root = root_stack[jnp.bitwise_xor(position, 1)]
            left_root = jnp.where(side_bit == 0, own_root, other_root)
            right_root = jnp.where(side_bit == 0, other_root, own_root)
            half_rows = lax.dynamic_slice_in_dim(left_root, (side_bit * (BS // 2)).astype(jnp.int32), BS // 2, 0)
            return product(product(half_rows, chosen), right_root)
        return (root_stack, lax.map(per_output, jnp.arange(N_TOK, dtype=jnp.int32)))
    root_stack, precond = lax.map(per_column, jnp.arange(N_BLK, dtype=jnp.int32))
    return (root_stack.transpose(1, 0, 2, 3), precond.transpose(1, 0, 2, 3))
```

```python
import math

import jax
import jax.numpy as jnp
from jax import lax
from jax.experimental import pallas as pl
from jax.experimental.pallas import tpu as pltpu
from jax.sharding import PartitionSpec as P

BETA = 0.9
DAMPING = 0.001
MESH = pl.DeviceIdType.MESH
BF = jnp.bfloat16
F32 = jnp.float32
X, Z_HI, Y, Z_LO, CORES = 4, 2, 8, 4, 2
BS = 512
HALF = 256
UNIT = 128
TOK = 1024
TH = 512
SHARD = 128
STEPS = 32767.0


def split(v):
    hi = v.astype(BF)
    lo = (v - hi.astype(F32)).astype(BF)
    return hi, lo


def dot(a, b):
    return jnp.dot(a, b, preferred_element_type=F32)


def dot_nt(a, b):
    return lax.dot_general(a, b, (((1,), (1,)), ((), ())), preferred_element_type=F32)


def mm3(a, b, d=dot):
    return d(a[0], b[0]) + (d(a[0], b[1]) + d(a[1], b[0]))


def encode(v):
    top = jnp.maximum(jnp.max(jnp.abs(v), axis=0, keepdims=True), 1e-30)
    code = jnp.round(v * (STEPS / top)).astype(jnp.int32).astype(jnp.int16)
    return code, top * (1.0 / STEPS)


def decode(code, step):
    return code.astype(jnp.int32).astype(F32) * step


def kernel(
    assign, grad, acts, stat_hbm, root_hbm, roots_out, precond_out,
    cols, rows, stat, root, hold, grad_full, ori, r2, r4, mat, upd, cur, upd2, tmp, mine, other, pre,
    xcs, xcr, xss, xsr, zcs, zcr, zss, zsr, acs, acr, ass_, asr, rcs, rcr, rss, rsr,
    loc_sem, ys, yr, sibs, sibr, ws, wr, xs, xr, zs, zr, as_, ar, rs, rr, out_sem,
):
    t = lax.axis_index("tok")
    j = lax.axis_index("blk")
    x = lax.rem(t, X)
    h = lax.div(t, X)
    core = lax.rem(j, CORES)
    y = lax.rem(lax.div(j, CORES), Y)
    w = lax.div(j, CORES * Y)

    def y_dev(d):
        return (t, w * (CORES * Y) + lax.rem(y + d + Y, Y) * CORES + core)

    def w_dev(d):
        return (t, lax.rem(w + d + Z_LO, Z_LO) * (CORES * Y) + y * CORES + core)

    def x_dev(d):
        return (h * X + lax.rem(x + d + X, X), j)

    sibling = (t, j + 1 - 2 * core)
    z_dev = ((1 - h) * X + x, j)
    pair_dev = (t + 1 - 2 * lax.rem(x, 2), j)

    partners = [sibling, z_dev] + [y_dev(d) for d in (1, -1)] + [w_dev(d) for d in (1, 2, 3)] + [x_dev(d) for d in (1, -1)]

    stat_in = pltpu.make_async_copy(stat_hbm, stat, loc_sem.at[0])
    root_in = pltpu.make_async_copy(root_hbm, root, loc_sem.at[1])
    root_in.start()
    stat_in.start()

    barrier = pltpu.get_barrier_semaphore()
    for dev in partners:
        pl.semaphore_signal(barrier, inc=1, device_id=dev, device_id_type=MESH)
    pl.semaphore_wait(barrier, len(partners))

    sends = []

    def remote(src, dst, ssem, rsem, dev):
        return pltpu.make_async_remote_copy(
            src_ref=src, dst_ref=dst, send_sem=ssem, recv_sem=rsem, device_id=dev, device_id_type=MESH
        )

    def start(src, dst, ssem, rsem, dev):
        copy = remote(src, dst, ssem, rsem, dev)
        copy.start()
        sends.append(copy)

    def landed(dst, ssem, rsem, dev):
        remote(dst, dst, ssem, rsem, dev).wait_recv()

    def shard(d, c):
        return lax.rem(y + d + Y, Y) * CORES + c

    def part(k):
        return pl.ds(k * TH, TH)

    own = shard(0, core)
    for k in range(2):
        for side, step in ((0, 1), (1, -1)):
            start(acts.at[part(k)], cols.at[own, part(k)], ys.at[side, 0, k], yr.at[side, 0, k], y_dev(step))
    for k in range(2):
        start(acts.at[part(k)], cols.at[own, part(k)], sibs.at[14 + k], sibr.at[14 + k], sibling)
    own_in = pltpu.make_async_copy(acts, cols.at[own], loc_sem.at[2])
    own_in.start()
    rows[w] = grad[...].T
    for d in (1, 2, 3):
        start(rows.at[w], rows.at[w], ws.at[d - 1], wr.at[d - 1], w_dev(d))

    root_in.wait()
    x0 = split(root[...])
    mine[0] = x0[0]
    mine[1] = x0[1]
    v = split(mm3(x0, x0))
    r2[0] = v[0]
    r2[1] = v[1]

    arrivals = []
    number = 0
    for d in (1, 2, 3, 4):
        for k in range(2):
            for side, step in ((0, 1), (1, -1)):
                if d == 4 and k != side:
                    continue
                region = cols.at[shard(-step * d, core), part(k)]
                landed(region, ys.at[side, d - 1, k], yr.at[side, d - 1, k], y_dev(-step))
                if d < 3 or (d == 3 and k == side):
                    start(region, region, ys.at[side, d, k], yr.at[side, d, k], y_dev(step))
                start(region, region, sibs.at[number], sibr.at[number], sibling)
                arrivals.append((shard(-step * d, 1 - core), k, number))
                number += 1

    for k in range(2):
        arrivals.append((shard(0, 1 - core), k, 14 + k))
    for index, k, n in arrivals:
        landed(cols.at[index, part(k)], sibs.at[n], sibr.at[n], sibling)
    own_in.wait()
    for d in (1, 2, 3):
        region = rows.at[lax.rem(w - d + Z_LO, Z_LO)]
        landed(region, ws.at[d - 1], wr.at[d - 1], w_dev(-d))

    scaling = 1.0 / math.sqrt(TOK * X * Z_HI)

    def piece(far, d):
        to_h = 1 - h if far == 0 else h
        to_x = lax.rem(x + d + X, X)
        pair = to_h * 2 + lax.div(to_x, 2)
        block = lax.div(assign[0, 2 * pair], 2)
        left = rows[pl.ds(2 * lax.rem(to_x, 2), 2)].reshape(HALF, TOK)
        right = jnp.concatenate([cols[4 * block + i] for i in range(4)], axis=1)
        return dot(left, right) * scaling

    def x_send(side, far, kind, value):
        code, step = encode(value)
        xcs[side, far, kind] = code
        xss[side, far, kind] = step
        dev = x_dev(1 if side == 0 else -1)
        start(xcs.at[side, far, kind], xcr.at[side, far, kind], xs.at[0, side, far, kind], xr.at[0, side, far, kind], dev)
        start(xss.at[side, far, kind], xsr.at[side, far, kind], xs.at[1, side, far, kind], xr.at[1, side, far, kind], dev)

    def x_recv(side, far, kind):
        dev = x_dev(-1 if side == 0 else 1)
        landed(xcr.at[side, far, kind], xs.at[0, side, far, kind], xr.at[0, side, far, kind], dev)
        landed(xsr.at[side, far, kind], xs.at[1, side, far, kind], xr.at[1, side, far, kind], dev)
        return decode(xcr[side, far, kind], xsr[side, far, kind])

    def first(far):
        v = piece(far, 2)
        x_send(0, far, 0, v[:UNIT])
        x_send(1, far, 0, v[UNIT:])

    def second(far):
        v = piece(far, 1)
        x_send(0, far, 1, v[UNIT:])
        hold[far, 0] = v[:UNIT]
        v = piece(far, -1)
        x_send(1, far, 1, v[:UNIT])
        hold[far, 1] = v[UNIT:]

    def third(far):
        x_send(0, far, 2, hold[far, 0] + x_recv(0, far, 0))
        x_send(1, far, 2, hold[far, 1] + x_recv(1, far, 0))

    def keep(far):
        v = piece(far, 0)
        hold[far, 2] = v[:UNIT]
        hold[far, 3] = v[UNIT:]

    def summed(far, u):
        if u == 0:
            return hold[far, 2] + x_recv(0, far, 2) + x_recv(1, far, 1)
        return hold[far, 3] + x_recv(0, far, 1) + x_recv(1, far, 2)

    first(0)
    second(0)
    first(1)
    third(0)
    second(1)
    keep(0)
    third(1)
    for u in range(2):
        code, step = encode(summed(0, u))
        zcs[u] = code
        zss[u] = step
        start(zcs.at[u], zcr.at[u], zs.at[0, u], zr.at[0, u], z_dev)
        start(zss.at[u], zsr.at[u], zs.at[1, u], zr.at[1, u], z_dev)
    keep(1)

    v = (r2[0], r2[1])
    v = split(mm3(v, v))
    r4[0] = v[0]
    r4[1] = v[1]

    low = 2 * lax.rem(x, 2)
    for u in range(2):
        v = summed(1, u)
        landed(zcr.at[u], zs.at[0, u], zr.at[0, u], z_dev)
        landed(zsr.at[u], zs.at[1, u], zr.at[1, u], z_dev)
        v = v + decode(zcr[u], zsr[u])
        code, step = encode(v)
        acs[u] = code
        ass_[u] = step
        start(acs.at[u], acr.at[u], as_.at[0, u], ar.at[0, u], pair_dev)
        start(ass_.at[u], asr.at[u], as_.at[1, u], ar.at[1, u], pair_dev)
        grad_full[low + u] = v
    for u in range(2):
        landed(acr.at[u], as_.at[0, u], ar.at[0, u], pair_dev)
        landed(asr.at[u], as_.at[1, u], ar.at[1, u], pair_dev)
        grad_full[2 - low + u] = decode(acr[u], asr[u])

    side_bit = lax.rem(assign[0, t], 2)
    g = grad_full[...].reshape(BS, BS)
    v = split(jnp.where(side_bit == 0, g, g.T))
    ori[0] = v[0]
    ori[1] = v[1]
    stat_in.wait()

    def eye(low_row, count):
        r = lax.broadcasted_iota(jnp.int32, (count, BS), 0) + low_row
        c = lax.broadcasted_iota(jnp.int32, (count, BS), 1)
        return r == c

    def both(ref):
        return ref[0], ref[1]

    def chunk(ref, q):
        return ref[0, pl.ds(q * HALF, HALF)], ref[1, pl.ds(q * HALF, HALF)]

    def put(ref, q, value):
        value = split(value)
        ref[0, pl.ds(q * HALF, HALF)] = value[0]
        ref[1, pl.ds(q * HALF, HALF)] = value[1]

    def update(value, q):
        return (jnp.where(eye(q * HALF, HALF), 5.0, 0.0) - value) * 0.25

    tokens = float(TOK * X * Z_HI)
    for q in range(2):
        square = mm3(chunk(ori, q), both(ori), dot_nt) * (1.0 / tokens)
        damp = jnp.where(eye(q * HALF, HALF), DAMPING, 0.0)
        put(tmp, q, BETA * stat[pl.ds(q * HALF, HALF)] + (1.0 - BETA) * square + damp)
    for q in range(2):
        v = mm3(chunk(r4, q), both(tmp))
        put(mat, q, v)
        put(upd, q, update(v, q))
    for q in range(2):
        put(upd2, q, mm3(chunk(upd, q), both(upd)))
    for q in range(2):
        put(cur, q, mm3(chunk(mine, q), both(upd)))
    for q in range(2):
        put(tmp, q, mm3(chunk(upd2, q), both(upd2)))
    for q in range(2):
        put(upd, q, update(mm3(chunk(tmp, q), both(mat)), q))
    outs = []
    for q in (1, 0):
        v = mm3(chunk(cur, q), both(upd))
        for i in range(2):
            u = 2 * q + i
            value = v[i * UNIT:(i + 1) * UNIT]
            on = eye(u * UNIT, UNIT)
            code, step = encode(jnp.where(on, 0.0, value))
            rcs[u] = code
            rss[u, 0:1] = step
            rss[u, 1:2] = jnp.sum(jnp.where(on, value, 0.0), axis=0, keepdims=True)
            start(rcs.at[u], rcr.at[u], rs.at[0, u], rr.at[0, u], pair_dev)
            start(rss.at[u], rsr.at[u], rs.at[1, u], rr.at[1, u], pair_dev)
        root[pl.ds(q * HALF, HALF)] = v
        copy = pltpu.make_async_copy(root.at[pl.ds(q * HALF, HALF)], roots_out.at[pl.ds(q * HALF, HALF)], out_sem.at[q])
        copy.start()
        outs.append(copy)
        put(mine, q, v)
    v = split(grad_full[...].reshape(BS, BS))
    ori[0] = v[0]
    ori[1] = v[1]

    def arrived(u):
        landed(rcr.at[u], rs.at[0, u], rr.at[0, u], pair_dev)
        landed(rsr.at[u], rs.at[1, u], rr.at[1, u], pair_dev)
        value = decode(rcr[u], rsr[u, 0:1]) + jnp.where(eye(u * UNIT, UNIT), rsr[u, 1:2], 0.0)
        value = split(value)
        other[0, pl.ds(u * UNIT, UNIT)] = value[0]
        other[1, pl.ds(u * UNIT, UNIT)] = value[1]

    arrived(2)
    arrived(3)
    half = tuple(
        jnp.where(side_bit == 0, a, b) for a, b in zip(chunk(mine, 0), chunk(other, 1))
    )
    v = split(mm3(half, both(ori)))
    pre[0] = v[0]
    pre[1] = v[1]
    arrived(0)
    arrived(1)
    right = tuple(jnp.where(side_bit == 0, b, a) for a, b in zip(both(mine), both(other)))
    final = mm3(both(pre), right)
    stat[pl.ds(0, HALF)] = final
    copy = pltpu.make_async_copy(stat.at[pl.ds(0, HALF)], precond_out, out_sem.at[2])
    copy.start()
    outs.append(copy)
    for copy in sends:
        copy.wait_send()
    for copy in outs:
        copy.wait()


def shards(grad_out, acts, stat_old, root_old, assign):
    def wide(*shape):
        return pltpu.VMEM((*shape, UNIT, BS), jnp.int16)

    def steps(*shape):
        return pltpu.VMEM((*shape, 1, BS), F32)

    def pair_of(rows_):
        return pltpu.VMEM((2, rows_, BS), BF)

    dma = pltpu.SemaphoreType.DMA
    anywhere = pl.BlockSpec(memory_space=pl.ANY)
    vmem = pl.BlockSpec(memory_space=pltpu.VMEM)
    roots, precond = pl.pallas_call(
        kernel,
        out_shape=(
            jax.ShapeDtypeStruct((BS, BS), F32),
            jax.ShapeDtypeStruct((HALF, BS), F32),
        ),
        in_specs=[pl.BlockSpec(memory_space=pltpu.SMEM), vmem, vmem, anywhere, anywhere],
        out_specs=(anywhere, anywhere),
        scratch_shapes=[
            pltpu.VMEM((CORES * Y, TOK, SHARD), BF),
            pltpu.VMEM((Z_LO, SHARD, TOK), BF),
            pltpu.VMEM((BS, BS), F32),
            pltpu.VMEM((BS, BS), F32),
            pltpu.VMEM((2, 4, UNIT, BS), F32),
            pltpu.VMEM((4, UNIT, BS), F32),
            *[pair_of(BS) for _ in range(10)],
            pair_of(HALF),
            wide(2, 2, 3), wide(2, 2, 3), steps(2, 2, 3), steps(2, 2, 3),
            wide(2), wide(2), steps(2), steps(2),
            wide(2), wide(2), steps(2), steps(2),
            wide(4), wide(4),
            pltpu.VMEM((4, 2, BS), F32), pltpu.VMEM((4, 2, BS), F32),
            dma((3,)),
            dma((2, 4, 2)), dma((2, 4, 2)),
            dma((16,)), dma((16,)),
            dma((3,)), dma((3,)),
            dma((2, 2, 2, 3)), dma((2, 2, 2, 3)),
            dma((2, 2)), dma((2, 2)),
            dma((2, 2)), dma((2, 2)),
            dma((2, 4)), dma((2, 4)),
            dma((3,)),
        ],
        compiler_params=pltpu.CompilerParams(
            collective_id=0, has_side_effects=True, vmem_limit_bytes=56 * 2**20
        ),
    )(assign, grad_out, acts, stat_old[0, 0], root_old[0, 0])
    return roots[None, None], precond[None, None]


def solution(mesh):
    placed = (
        P("tok", "blk"),
        P("tok", "blk"),
        P("tok", "blk", None, None),
        P("tok", "blk", None, None),
        P("blk", None),
    )
    return jax.shard_map(
        shards,
        mesh=mesh,
        in_specs=placed,
        out_specs=(P("tok", "blk", None, None), P("tok", "blk", None, None)),
        check_vma=False,
    )
```

```python
import math

import jax
import jax.numpy as jnp
from jax import lax
from jax.experimental import pallas as pl
from jax.experimental.pallas import tpu as pltpu
from jax.sharding import PartitionSpec as P

BETA = 0.9
DAMPING = 0.001
MESH = pl.DeviceIdType.MESH
BF = jnp.bfloat16
F32 = jnp.float32
X, Z_HI, Y, Z_LO, CORES = 4, 2, 8, 4, 2
BS = 512
HALF = 256
UNIT = 128
TOK = 1024
QT = 256
SUB = 32
OFFSETS = (0, 1, -1, 2, -2, 3, -3, 4)
TURNS = (2, 1, -1, 0)
RIGHTWARD = (0, 1, 3, 5)
STRAIGHT = 7
SHARD = 128
STEPS = 32767.0


def split(v):
    hi = v.astype(BF)
    lo = (v - hi.astype(F32)).astype(BF)
    return hi, lo


def dot(a, b):
    return jnp.dot(a, b, preferred_element_type=F32)


def dot_nt(a, b):
    return lax.dot_general(a, b, (((1,), (1,)), ((), ())), preferred_element_type=F32)


def mm3(a, b, d=dot):
    return d(a[0], b[0]) + (d(a[0], b[1]) + d(a[1], b[0]))


def encode(v):
    top = jnp.maximum(jnp.max(jnp.abs(v), axis=0, keepdims=True), 1e-30)
    code = jnp.round(v * (STEPS / top)).astype(jnp.int32).astype(jnp.int16)
    return code, top * (1.0 / STEPS)


def decode(code, step):
    return code.astype(jnp.int32).astype(F32) * step


def kernel(
    assign, grad, acts, stat_hbm, root_hbm, roots_out, precond_out,
    cols, rows, stat, root, hold, grad_full, ori, r2, r4, mat, upd, cur, upd2, tmp, mine, other, pre,
    xcs, xcr, xss, xsr, zcs, zcr, zss, zsr, acs, acr, ass_, asr, rcs, rcr, rss, rsr,
    loc_sem, ys, yr, sibs, sibr, ws, wr, xs, xr, zs, zr, as_, ar, rs, rr,
):
    t = lax.axis_index("tok")
    j = lax.axis_index("blk")
    x = lax.rem(t, X)
    h = lax.div(t, X)
    core = lax.rem(j, CORES)
    y = lax.rem(lax.div(j, CORES), Y)
    w = lax.div(j, CORES * Y)

    def y_dev(d):
        return (t, w * (CORES * Y) + lax.rem(y + d + Y, Y) * CORES + core)

    def w_dev(d):
        return (t, lax.rem(w + d + Z_LO, Z_LO) * (CORES * Y) + y * CORES + core)

    def x_dev(d):
        return (h * X + lax.rem(x + d + X, X), j)

    sibling = (t, j + 1 - 2 * core)
    z_dev = ((1 - h) * X + x, j)
    pair_dev = (t + 1 - 2 * lax.rem(x, 2), j)

    partners = [sibling, z_dev] + [y_dev(d) for d in (1, -1)]
    partners += [dev(d) for dev in (w_dev, x_dev) for d in (1, 2, 3)]

    stat_in = pltpu.make_async_copy(stat_hbm, stat, loc_sem.at[0])
    root_in = pltpu.make_async_copy(root_hbm, root, loc_sem.at[1])
    root_in.start()
    stat_in.start()

    barrier = pltpu.get_barrier_semaphore()
    for dev in partners:
        pl.semaphore_signal(barrier, inc=1, device_id=dev, device_id_type=MESH)
    pl.semaphore_wait(barrier, len(partners))

    sends = []

    def remote(src, dst, ssem, rsem, dev):
        return pltpu.make_async_remote_copy(
            src_ref=src, dst_ref=dst, send_sem=ssem, recv_sem=rsem, device_id=dev, device_id_type=MESH
        )

    def start(src, dst, ssem, rsem, dev):
        copy = remote(src, dst, ssem, rsem, dev)
        copy.start()
        sends.append(copy)

    def landed(dst, ssem, rsem, dev):
        remote(dst, dst, ssem, rsem, dev).wait_recv()

    def at_y(d):
        return lax.rem(y + d + Y, Y)

    SIDES = ((0, 1), (1, -1))

    def part(q):
        return pl.ds(q * QT, QT)

    def ring(d):
        return [((n + 2 * side) % 4, side, step) for n in range(4 if d < 4 else 2) for side, step in SIDES]

    def number(d, q, side):
        return 24 + q if d == 4 else ((d - 1) * 4 + q) * 2 + side

    def y_step(d, parts):
        for q, side, step in ring(d):
            if (q + 2 * side) % 4 not in parts:
                continue
            region = cols.at[at_y(-step * d) * CORES + core, part(q)]
            landed(region, ys.at[side, d - 1, q], yr.at[side, d - 1, q], y_dev(-step))
            if d < 3 or (d == 3 and q // 2 == side):
                start(region, region, ys.at[side, d, q], yr.at[side, d, q], y_dev(step))
            n = number(d, q, side)
            start(region, region, sibs.at[n], sibr.at[n], sibling)

    def y_ready(d):
        if d == 0:
            own_in.wait()
            landed(cols.at[y * CORES + 1 - core], sibs.at[28], sibr.at[28], sibling)
            return
        for q, side, step in ring(d):
            n = number(d, q, side)
            landed(cols.at[at_y(-step * d) * CORES + 1 - core, part(q)], sibs.at[n], sibr.at[n], sibling)

    def quarter(e):
        return lax.rem(x + TURNS[e] + X, X)

    def rows_ready(e):
        for d in (2, 3, 1):
            unit = rows.at[quarter(e), lax.rem(w - d + Z_LO, Z_LO)]
            landed(unit, ws.at[e, d - 1], wr.at[e, d - 1], w_dev(-d))

    for q, side, step in ring(0):
        start(acts.at[part(q)], cols.at[y * CORES + core, part(q)], ys.at[side, 0, q], yr.at[side, 0, q], y_dev(step))
    start(acts, cols.at[y * CORES + core], sibs.at[28], sibr.at[28], sibling)
    own_in = pltpu.make_async_copy(acts, cols.at[y * CORES + core], loc_sem.at[2])
    own_in.start()
    v = grad[...].T
    for q in range(4):
        rows[q, w] = v[q * SUB:(q + 1) * SUB]

    def rows_send(e):
        unit = rows.at[quarter(e), w]
        for d in (2, 3, 1):
            start(unit, unit, ws.at[e, d - 1], wr.at[e, d - 1], w_dev(d))

    rows_send(0)
    root_in.wait()
    x0 = split(root[...])
    mine[0] = x0[0]
    mine[1] = x0[1]
    v = split(mm3(x0, x0))
    r2[0] = v[0]
    r2[1] = v[1]
    v = split(mm3(v, v))
    r4[0] = v[0]
    r4[1] = v[1]

    scaling = 1.0 / math.sqrt(TOK * X * Z_HI)

    def piece(e, g):
        left = rows[quarter(e)].reshape(UNIT, TOK)
        at = at_y(OFFSETS[g]) * CORES
        right = jnp.concatenate([cols[at], cols[at + 1]], axis=1)
        return dot(left, right) * scaling

    RIGHT, LEFT, FAR = 0, 1, 2

    def heading(slot, g):
        if slot == FAR:
            return 2 if g == STRAIGHT else (1 if g in RIGHTWARD else -1)
        return 1 if slot == RIGHT else -1

    def x_send(slot, g, value):
        code, step = encode(value)
        xcs[slot, g] = code
        xss[slot, g] = step
        dev = x_dev(heading(slot, g))
        start(xcs.at[slot, g], xcr.at[slot, g], xs.at[0, slot, g], xr.at[0, slot, g], dev)
        start(xss.at[slot, g], xsr.at[slot, g], xs.at[1, slot, g], xr.at[1, slot, g], dev)

    def x_take(slot, g):
        dev = x_dev(-heading(slot, g))
        landed(xcr.at[slot, g], xs.at[0, slot, g], xr.at[0, slot, g], dev)
        landed(xsr.at[slot, g], xs.at[1, slot, g], xr.at[1, slot, g], dev)
        return decode(xcr[slot, g], xsr[slot, g])

    def far(*gs):
        for g in gs:
            x_send(FAR, g, piece(0, g))

    def raw(slot, *gs):
        for g in gs:
            x_send(slot, g, piece(slot + 1, g))

    def add(slot, *gs):
        for g in gs:
            x_send(slot, g, piece(slot + 1, g) + x_take(FAR, g))

    y_step(1, (0, 1))
    rows_send(1)
    y_step(1, (2, 3))
    y_ready(0)
    y_ready(1)
    rows_ready(0)
    far(0, 2, 1)
    y_step(2, (0, 1))
    rows_send(2)
    y_step(2, (2, 3))
    y_ready(2)
    far(3, 4)
    rows_ready(1)
    rows_send(3)
    raw(RIGHT, 2)
    add(RIGHT, 0)
    y_step(3, (0, 1))
    raw(RIGHT, 4)
    add(RIGHT, 1)
    y_step(3, (2, 3))
    rows_ready(2)
    raw(LEFT, 0, 1)
    add(LEFT, 2)
    y_ready(3)
    far(5, 6)
    raw(LEFT, 3)
    add(LEFT, 4)
    y_step(4, (0, 1))
    add(RIGHT, 3)
    raw(RIGHT, 6)
    raw(LEFT, 5)
    y_ready(4)
    far(7)
    raw(LEFT, 7)
    raw(RIGHT, 7)
    add(RIGHT, 5)
    add(LEFT, 6)
    rows_ready(3)
    for g in range(8):
        hold[at_y(OFFSETS[g])] = piece(3, g)

    for g in range(8):
        where = at_y(OFFSETS[g])
        v = hold[where] + x_take(RIGHT, g) + x_take(LEFT, g)
        hold[where] = v + x_take(FAR, g) if g == STRAIGHT else v

    mine_pair = lax.div(x, 2)

    def block(to_h, i, c):
        pair = to_h * 2 + (1 - mine_pair if i == 0 else mine_pair)
        return hold[2 * lax.div(assign[0, 2 * pair], 2) + c]

    UNITS = [(i, c) for i in range(2) for c in range(2)]
    for i, c in UNITS:
        code, step = encode(block(1 - h, i, c))
        zcs[i, c] = code
        zss[i, c] = step
        start(zcs.at[i, c], zcr.at[i, c], zs.at[0, i, c], zr.at[0, i, c], z_dev)
        start(zss.at[i, c], zsr.at[i, c], zs.at[1, i, c], zr.at[1, i, c], z_dev)

    near = 1 - 2 * lax.rem(x, 2)
    across = [(0, near, 1), (1, 2, 0), (2, -near, 0)]

    def place(where, c, value):
        for q in range(4):
            grad_full[q, where, :, c * HALF:(c + 1) * HALF] = value[q * SUB:(q + 1) * SUB]

    for i, c in UNITS:
        landed(zcr.at[i, c], zs.at[0, i, c], zr.at[0, i, c], z_dev)
        landed(zsr.at[i, c], zs.at[1, i, c], zr.at[1, i, c], z_dev)
        v = block(h, i, c) + decode(zcr[i, c], zsr[i, c])
        code, step = encode(v)
        acs[i, c] = code
        ass_[i, c] = step
        for n, d, unit in across:
            if unit == i:
                start(acs.at[i, c], acr.at[n, c], as_.at[0, n, c], ar.at[0, n, c], x_dev(d))
                start(ass_.at[i, c], asr.at[n, c], as_.at[1, n, c], ar.at[1, n, c], x_dev(d))
        if i == 1:
            place(x, c, v)
    for n, d, unit in (across[1], across[2], across[0]):
        for c in range(2):
            landed(acr.at[n, c], as_.at[0, n, c], ar.at[0, n, c], x_dev(d))
            landed(asr.at[n, c], as_.at[1, n, c], ar.at[1, n, c], x_dev(d))
            place(lax.rem(x + d + X, X), c, decode(acr[n, c], asr[n, c]))

    side_bit = lax.rem(assign[0, t], 2)
    g = grad_full[...].reshape(BS, BS)
    v = split(jnp.where(side_bit == 0, g, g.T))
    ori[0] = v[0]
    ori[1] = v[1]
    stat_in.wait()

    def eye(low_row, count):
        r = lax.broadcasted_iota(jnp.int32, (count, BS), 0) + low_row
        c = lax.broadcasted_iota(jnp.int32, (count, BS), 1)
        return r == c

    def both(ref):
        return ref[0], ref[1]

    def chunk(ref, q):
        return ref[0, pl.ds(q * HALF, HALF)], ref[1, pl.ds(q * HALF, HALF)]

    def put(ref, q, value):
        value = split(value)
        ref[0, pl.ds(q * HALF, HALF)] = value[0]
        ref[1, pl.ds(q * HALF, HALF)] = value[1]

    def update(value, q):
        return (jnp.where(eye(q * HALF, HALF), 5.0, 0.0) - value) * 0.25

    tokens = float(TOK * X * Z_HI)
    for q in range(2):
        square = mm3(chunk(ori, q), both(ori), dot_nt) * (1.0 / tokens)
        damp = jnp.where(eye(q * HALF, HALF), DAMPING, 0.0)
        put(tmp, q, BETA * stat[pl.ds(q * HALF, HALF)] + (1.0 - BETA) * square + damp)
    for q in range(2):
        v = mm3(chunk(r4, q), both(tmp))
        put(mat, q, v)
        put(upd, q, update(v, q))
    for q in range(2):
        put(upd2, q, mm3(chunk(upd, q), both(upd)))
    for q in range(2):
        put(cur, q, mm3(chunk(mine, q), both(upd)))
    for q in range(2):
        put(tmp, q, mm3(chunk(upd2, q), both(upd2)))
    for q in range(2):
        put(upd, q, update(mm3(chunk(tmp, q), both(mat)), q))
    for q in (1, 0):
        v = mm3(chunk(cur, q), both(upd))
        for i in range(2):
            u = 2 * q + i
            value = v[i * UNIT:(i + 1) * UNIT]
            on = eye(u * UNIT, UNIT)
            code, step = encode(jnp.where(on, 0.0, value))
            rcs[u] = code
            rss[u, 0:1] = step
            rss[u, 1:2] = jnp.sum(jnp.where(on, value, 0.0), axis=0, keepdims=True)
            start(rcs.at[u], rcr.at[u], rs.at[0, u], rr.at[0, u], pair_dev)
            start(rss.at[u], rsr.at[u], rs.at[1, u], rr.at[1, u], pair_dev)
        roots_out[pl.ds(q * HALF, HALF)] = v
        put(mine, q, v)
    v = split(grad_full[...].reshape(BS, BS))
    ori[0] = v[0]
    ori[1] = v[1]

    def arrived(u):
        landed(rcr.at[u], rs.at[0, u], rr.at[0, u], pair_dev)
        landed(rsr.at[u], rs.at[1, u], rr.at[1, u], pair_dev)
        value = decode(rcr[u], rsr[u, 0:1]) + jnp.where(eye(u * UNIT, UNIT), rsr[u, 1:2], 0.0)
        value = split(value)
        other[0, pl.ds(u * UNIT, UNIT)] = value[0]
        other[1, pl.ds(u * UNIT, UNIT)] = value[1]

    arrived(2)
    arrived(3)
    half = tuple(
        jnp.where(side_bit == 0, a, b) for a, b in zip(chunk(mine, 0), chunk(other, 1))
    )
    v = split(mm3(half, both(ori)))
    pre[0] = v[0]
    pre[1] = v[1]
    arrived(0)
    arrived(1)
    right = tuple(jnp.where(side_bit == 0, b, a) for a, b in zip(both(mine), both(other)))
    precond_out[...] = mm3(both(pre), right)
    for copy in sends:
        copy.wait_send()


def shards(grad_out, acts, stat_old, root_old, assign):
    def wide(*shape):
        return pltpu.VMEM((*shape, UNIT, BS), jnp.int16)

    def narrow(*shape):
        return pltpu.VMEM((*shape, UNIT, HALF), jnp.int16)

    def steps(count, *shape):
        return pltpu.VMEM((*shape, 1, count), F32)

    def pair_of(rows_):
        return pltpu.VMEM((2, rows_, BS), BF)

    dma = pltpu.SemaphoreType.DMA
    anywhere = pl.BlockSpec(memory_space=pl.ANY)
    vmem = pl.BlockSpec(memory_space=pltpu.VMEM)
    roots, precond = pl.pallas_call(
        kernel,
        out_shape=(
            pltpu.VMEM((BS, BS), F32),
            pltpu.VMEM((HALF, BS), F32),
        ),
        in_specs=[pl.BlockSpec(memory_space=pltpu.SMEM), vmem, vmem, anywhere, anywhere],
        out_specs=(vmem, vmem),
        scratch_shapes=[
            pltpu.VMEM((CORES * Y, TOK, SHARD), BF),
            pltpu.VMEM((X, Z_LO, SUB, TOK), BF),
            pltpu.VMEM((BS, BS), F32),
            pltpu.VMEM((BS, BS), F32),
            pltpu.VMEM((Y, UNIT, HALF), F32),
            pltpu.VMEM((Z_LO, X, SUB, BS), F32),
            *[pair_of(BS) for _ in range(10)],
            pair_of(HALF),
            narrow(3, Y), narrow(3, Y), steps(HALF, 3, Y), steps(HALF, 3, Y),
            narrow(2, 2), narrow(2, 2), steps(HALF, 2, 2), steps(HALF, 2, 2),
            narrow(2, 2), narrow(3, 2), steps(HALF, 2, 2), steps(HALF, 3, 2),
            wide(4), wide(4),
            pltpu.VMEM((4, 2, BS), F32), pltpu.VMEM((4, 2, BS), F32),
            dma((3,)),
            dma((2, 4, 4)), dma((2, 4, 4)),
            dma((29,)), dma((29,)),
            dma((4, 3)), dma((4, 3)),
            dma((2, 3, Y)), dma((2, 3, Y)),
            dma((2, 2, 2)), dma((2, 2, 2)),
            dma((2, 3, 2)), dma((2, 3, 2)),
            dma((2, 4)), dma((2, 4)),
        ],
        compiler_params=pltpu.CompilerParams(
            collective_id=0, has_side_effects=True, vmem_limit_bytes=56 * 2**20
        ),
    )(assign, grad_out, acts, stat_old[0, 0], root_old[0, 0])
    return roots[None, None], precond[None, None]


def solution(mesh):
    placed = (
        P("tok", "blk"),
        P("tok", "blk"),
        P("tok", "blk", None, None),
        P("tok", "blk", None, None),
        P("blk", None),
    )
    return jax.shard_map(
        shards,
        mesh=mesh,
        in_specs=placed,
        out_specs=(P("tok", "blk", None, None), P("tok", "blk", None, None)),
        check_vma=False,
    )
```

```python
import math

import jax
import jax.numpy as jnp
from jax import lax
from jax.experimental import pallas as pl
from jax.experimental.pallas import tpu as pltpu
from jax.sharding import PartitionSpec as P

BETA = 0.9
DAMPING = 0.001
MESH = pl.DeviceIdType.MESH
BF = jnp.bfloat16
F32 = jnp.float32
X, Z_HI, Y, Z_LO, CORES = 4, 2, 8, 4, 2
BS = 512
HALF = 256
UNIT = 128
TOK = 1024
QT = 256
SUB = 32
OFFSETS = (0, 1, -1, 2, -2, 3, -3, 4)
TURNS = (2, 1, -1, 0)
RIGHTWARD = (0, 1, 3, 5)
STRAIGHT = 7
SHARD = 128
STEPS = 32767.0


def split(v):
    hi = v.astype(BF)
    lo = (v - hi.astype(F32)).astype(BF)
    return hi, lo


def dot(a, b):
    return jnp.dot(a, b, preferred_element_type=F32)


def dot_nt(a, b):
    return lax.dot_general(a, b, (((1,), (1,)), ((), ())), preferred_element_type=F32)


def mm3(a, b, d=dot):
    return d(a[0], b[0]) + (d(a[0], b[1]) + d(a[1], b[0]))


def encode(v):
    top = jnp.maximum(jnp.max(jnp.abs(v), axis=0, keepdims=True), 1e-30)
    code = jnp.round(v * (STEPS / top)).astype(jnp.int32).astype(jnp.int16)
    return code, top * (1.0 / STEPS)


def decode(code, step):
    return code.astype(jnp.int32).astype(F32) * step


def kernel(
    assign, grad, acts, stat_hbm, root_hbm, roots_out, precond_out,
    cols, rows, stat, root, hold, grad_full, ori, r2, r4, mat, upd, cur, upd2, tmp, mine, other, pre,
    ori_b, r4_b, mat_b, upd_b, cur_b, upd2_b, tmp_b, old_b, stat_b,
    xcs, xcr, xss, xsr, zcs, zcr, zss, zsr, acs, acr, ass_, asr, rcs, rcr, rss, rsr,
    loc_sem, ys, yr, sibs, sibr, ws, wr, xs, xr, zs, zr, as_, ar, rs, rr,
):
    t = lax.axis_index("tok")
    j = lax.axis_index("blk")
    x = lax.rem(t, X)
    h = lax.div(t, X)
    core = lax.rem(j, CORES)
    y = lax.rem(lax.div(j, CORES), Y)
    w = lax.div(j, CORES * Y)

    def y_dev(d):
        return (t, w * (CORES * Y) + lax.rem(y + d + Y, Y) * CORES + core)

    def w_dev(d):
        return (t, lax.rem(w + d + Z_LO, Z_LO) * (CORES * Y) + y * CORES + core)

    def x_dev(d):
        return (h * X + lax.rem(x + d + X, X), j)

    sibling = (t, j + 1 - 2 * core)
    z_dev = ((1 - h) * X + x, j)
    pair_dev = (t + 1 - 2 * lax.rem(x, 2), j)

    partners = [sibling, z_dev] + [y_dev(d) for d in (1, -1)]
    partners += [dev(d) for dev in (w_dev, x_dev) for d in (1, 2, 3)]

    stat_in = pltpu.make_async_copy(stat_hbm, stat, loc_sem.at[0])
    root_in = pltpu.make_async_copy(root_hbm, root, loc_sem.at[1])
    root_in.start()
    stat_in.start()

    barrier = pltpu.get_barrier_semaphore()
    for dev in partners:
        pl.semaphore_signal(barrier, inc=1, device_id=dev, device_id_type=MESH)
    pl.semaphore_wait(barrier, len(partners))

    sends = []

    def remote(src, dst, ssem, rsem, dev):
        return pltpu.make_async_remote_copy(
            src_ref=src, dst_ref=dst, send_sem=ssem, recv_sem=rsem, device_id=dev, device_id_type=MESH
        )

    def start(src, dst, ssem, rsem, dev):
        copy = remote(src, dst, ssem, rsem, dev)
        copy.start()
        sends.append(copy)

    def landed(dst, ssem, rsem, dev):
        remote(dst, dst, ssem, rsem, dev).wait_recv()

    def at_y(d):
        return lax.rem(y + d + Y, Y)

    SIDES = ((0, 1), (1, -1))

    def part(q):
        return pl.ds(q * QT, QT)

    def ring(d):
        return [((n + 2 * side) % 4, side, step) for n in range(4 if d < 4 else 2) for side, step in SIDES]

    def number(d, q, side):
        return 24 + q if d == 4 else ((d - 1) * 4 + q) * 2 + side

    def y_step(d, parts):
        for q, side, step in ring(d):
            if (q + 2 * side) % 4 not in parts:
                continue
            region = cols.at[at_y(-step * d) * CORES + core, part(q)]
            landed(region, ys.at[side, d - 1, q], yr.at[side, d - 1, q], y_dev(-step))
            if d < 3 or (d == 3 and q // 2 == side):
                start(region, region, ys.at[side, d, q], yr.at[side, d, q], y_dev(step))
            n = number(d, q, side)
            start(region, region, sibs.at[n], sibr.at[n], sibling)

    def y_ready(d):
        if d == 0:
            own_in.wait()
            landed(cols.at[y * CORES + 1 - core], sibs.at[28], sibr.at[28], sibling)
            return
        for q, side, step in ring(d):
            n = number(d, q, side)
            landed(cols.at[at_y(-step * d) * CORES + 1 - core, part(q)], sibs.at[n], sibr.at[n], sibling)

    def quarter(e):
        return lax.rem(x + TURNS[e] + X, X)

    def rows_ready(e):
        for d in (2, 3, 1):
            unit = rows.at[quarter(e), lax.rem(w - d + Z_LO, Z_LO)]
            landed(unit, ws.at[e, d - 1], wr.at[e, d - 1], w_dev(-d))

    for q, side, step in ring(0):
        start(acts.at[part(q)], cols.at[y * CORES + core, part(q)], ys.at[side, 0, q], yr.at[side, 0, q], y_dev(step))
    start(acts, cols.at[y * CORES + core], sibs.at[28], sibr.at[28], sibling)
    own_in = pltpu.make_async_copy(acts, cols.at[y * CORES + core], loc_sem.at[2])
    own_in.start()
    v = grad[...].T
    for q in range(4):
        rows[q, w] = v[q * SUB:(q + 1) * SUB]

    def rows_send(e):
        unit = rows.at[quarter(e), w]
        for d in (2, 3, 1):
            start(unit, unit, ws.at[e, d - 1], wr.at[e, d - 1], w_dev(d))

    rows_send(0)
    def eye(low_row, count):
        r = lax.broadcasted_iota(jnp.int32, (count, BS), 0) + low_row
        c = lax.broadcasted_iota(jnp.int32, (count, BS), 1)
        return r == c

    def old_send(n, ref):
        for u in range(4):
            value = ref[pl.ds(u * UNIT, UNIT)]
            on = eye(u * UNIT, UNIT)
            code, step = encode(jnp.where(on, 0.0, value))
            rcs[n, u] = code
            rss[n, u, 0:1] = step
            rss[n, u, 1:2] = jnp.sum(jnp.where(on, value, 0.0), axis=0, keepdims=True)
        start(rcs.at[n], rcr.at[n], rs.at[0, n], rr.at[0, n], pair_dev)
        start(rss.at[n], rsr.at[n], rs.at[1, n], rr.at[1, n], pair_dev)

    def old_landed(n):
        landed(rcr.at[n], rs.at[0, n], rr.at[0, n], pair_dev)
        landed(rsr.at[n], rs.at[1, n], rr.at[1, n], pair_dev)

    def old_take(n, u):
        return decode(rcr[n, u], rsr[n, u, 0:1]) + jnp.where(eye(u * UNIT, UNIT), rsr[n, u, 1:2], 0.0)

    root_in.wait()
    old_send(0, root)
    x0 = split(root[...])
    mine[0] = x0[0]
    mine[1] = x0[1]
    v = split(mm3(x0, x0))
    r2[0] = v[0]
    r2[1] = v[1]
    v = split(mm3(v, v))
    r4[0] = v[0]
    r4[1] = v[1]

    scaling = 1.0 / math.sqrt(TOK * X * Z_HI)

    def piece(e, g):
        left = rows[quarter(e)].reshape(UNIT, TOK)
        at = at_y(OFFSETS[g]) * CORES
        right = jnp.concatenate([cols[at], cols[at + 1]], axis=1)
        return dot(left, right) * scaling

    RIGHT, LEFT, FAR = 0, 1, 2

    def heading(slot, g):
        if slot == FAR:
            return 2 if g == STRAIGHT else (1 if g in RIGHTWARD else -1)
        return 1 if slot == RIGHT else -1

    def x_send(slot, g, value):
        code, step = encode(value)
        xcs[slot, g] = code
        xss[slot, g] = step
        dev = x_dev(heading(slot, g))
        start(xcs.at[slot, g], xcr.at[slot, g], xs.at[0, slot, g], xr.at[0, slot, g], dev)
        start(xss.at[slot, g], xsr.at[slot, g], xs.at[1, slot, g], xr.at[1, slot, g], dev)

    def x_take(slot, g):
        dev = x_dev(-heading(slot, g))
        landed(xcr.at[slot, g], xs.at[0, slot, g], xr.at[0, slot, g], dev)
        landed(xsr.at[slot, g], xs.at[1, slot, g], xr.at[1, slot, g], dev)
        return decode(xcr[slot, g], xsr[slot, g])

    def far(*gs):
        for g in gs:
            x_send(FAR, g, piece(0, g))

    def raw(slot, *gs):
        for g in gs:
            x_send(slot, g, piece(slot + 1, g))

    def add(slot, *gs):
        for g in gs:
            x_send(slot, g, piece(slot + 1, g) + x_take(FAR, g))

    y_step(1, (0, 1))
    rows_send(1)
    y_step(1, (2, 3))
    y_ready(0)
    y_ready(1)
    rows_ready(0)
    far(0, 2, 1)
    y_step(2, (0, 1))
    rows_send(2)
    y_step(2, (2, 3))
    y_ready(2)
    far(3, 4)
    rows_ready(1)
    rows_send(3)
    raw(RIGHT, 2)
    add(RIGHT, 0)
    y_step(3, (0, 1))
    raw(RIGHT, 4)
    add(RIGHT, 1)
    y_step(3, (2, 3))
    rows_ready(2)
    raw(LEFT, 0, 1)
    add(LEFT, 2)
    y_ready(3)
    far(5, 6)
    raw(LEFT, 3)
    add(LEFT, 4)
    y_step(4, (0, 1))
    add(RIGHT, 3)
    raw(RIGHT, 6)
    raw(LEFT, 5)
    add(RIGHT, 5)
    add(LEFT, 6)
    y_ready(4)
    far(7)
    raw(LEFT, 7)
    raw(RIGHT, 7)
    stat_in.wait()
    old_send(1, stat)
    rows_ready(3)
    for g in range(8):
        hold[at_y(OFFSETS[g])] = piece(3, g)

    for g in range(8):
        where = at_y(OFFSETS[g])
        v = hold[where] + x_take(RIGHT, g) + x_take(LEFT, g)
        hold[where] = v + x_take(FAR, g) if g == STRAIGHT else v

    mine_pair = lax.div(x, 2)

    def block(to_h, i, c):
        pair = to_h * 2 + (1 - mine_pair if i == 0 else mine_pair)
        return hold[2 * lax.div(assign[0, 2 * pair], 2) + c]

    UNITS = [(i, c) for i in range(2) for c in range(2)]
    for i, c in UNITS:
        code, step = encode(block(1 - h, i, c))
        zcs[i, c] = code
        zss[i, c] = step
        start(zcs.at[i, c], zcr.at[i, c], zs.at[0, i, c], zr.at[0, i, c], z_dev)
        start(zss.at[i, c], zsr.at[i, c], zs.at[1, i, c], zr.at[1, i, c], z_dev)

    old_landed(0)
    for u in range(4):
        v = split(old_take(0, u))
        old_b[0, pl.ds(u * UNIT, UNIT)] = v[0]
        old_b[1, pl.ds(u * UNIT, UNIT)] = v[1]
    v = (old_b[0], old_b[1])
    v = split(mm3(v, v))
    v = split(mm3(v, v))
    r4_b[0] = v[0]
    r4_b[1] = v[1]

    near = 1 - 2 * lax.rem(x, 2)
    across = [(0, near, 1), (1, 2, 0), (2, -near, 0)]

    def place(where, c, value):
        for q in range(4):
            grad_full[q, where, :, c * HALF:(c + 1) * HALF] = value[q * SUB:(q + 1) * SUB]

    for i, c in UNITS:
        landed(zcr.at[i, c], zs.at[0, i, c], zr.at[0, i, c], z_dev)
        landed(zsr.at[i, c], zs.at[1, i, c], zr.at[1, i, c], z_dev)
        v = block(h, i, c) + decode(zcr[i, c], zsr[i, c])
        code, step = encode(v)
        acs[i, c] = code
        ass_[i, c] = step
        for n, d, unit in across:
            if unit == i:
                start(acs.at[i, c], acr.at[n, c], as_.at[0, n, c], ar.at[0, n, c], x_dev(d))
                start(ass_.at[i, c], asr.at[n, c], as_.at[1, n, c], ar.at[1, n, c], x_dev(d))
        if i == 1:
            place(x, c, v)
    old_landed(1)
    for u in range(4):
        stat_b[pl.ds(u * UNIT, UNIT)] = old_take(1, u)
    for n, d, unit in (across[1], across[2], across[0]):
        for c in range(2):
            landed(acr.at[n, c], as_.at[0, n, c], ar.at[0, n, c], x_dev(d))
            landed(asr.at[n, c], as_.at[1, n, c], ar.at[1, n, c], x_dev(d))
            place(lax.rem(x + d + X, X), c, decode(acr[n, c], asr[n, c]))

    side_bit = lax.rem(assign[0, t], 2)
    g = grad_full[...].reshape(BS, BS)
    gt = g.T
    for ref, value in ((ori, jnp.where(side_bit == 0, g, gt)), (ori_b, jnp.where(side_bit == 0, gt, g))):
        v = split(value)
        ref[0] = v[0]
        ref[1] = v[1]

    def both(ref):
        return ref[0], ref[1]

    def chunk(ref, q):
        return ref[0, pl.ds(q * HALF, HALF)], ref[1, pl.ds(q * HALF, HALF)]

    def put(ref, q, value):
        value = split(value)
        ref[0, pl.ds(q * HALF, HALF)] = value[0]
        ref[1, pl.ds(q * HALF, HALF)] = value[1]

    def update(value, q):
        return (jnp.where(eye(q * HALF, HALF), 5.0, 0.0) - value) * 0.25

    tokens = float(TOK * X * Z_HI)
    own_set = (ori, r4, mat, upd, cur, upd2, tmp, mine, stat)
    other_set = (ori_b, r4_b, mat_b, upd_b, cur_b, upd2_b, tmp_b, old_b, stat_b)
    sets = (own_set, other_set)
    halves = range(2)
    for ori_, r4_, mat_, upd_, cur_, upd2_, tmp_, old_, stat_ in sets:
        for q in halves:
            square = mm3(chunk(ori_, q), both(ori_), dot_nt) * (1.0 / tokens)
            damp = jnp.where(eye(q * HALF, HALF), DAMPING, 0.0)
            put(tmp_, q, BETA * stat_[pl.ds(q * HALF, HALF)] + (1.0 - BETA) * square + damp)
    for ori_, r4_, mat_, upd_, cur_, upd2_, tmp_, old_, stat_ in sets:
        for q in halves:
            v = mm3(chunk(r4_, q), both(tmp_))
            put(mat_, q, v)
            put(upd_, q, update(v, q))
    for ori_, r4_, mat_, upd_, cur_, upd2_, tmp_, old_, stat_ in sets:
        for q in halves:
            put(upd2_, q, mm3(chunk(upd_, q), both(upd_)))
        for q in halves:
            put(cur_, q, mm3(chunk(old_, q), both(upd_)))
    for ori_, r4_, mat_, upd_, cur_, upd2_, tmp_, old_, stat_ in sets:
        for q in halves:
            put(tmp_, q, mm3(chunk(upd2_, q), both(upd2_)))
    for ori_, r4_, mat_, upd_, cur_, upd2_, tmp_, old_, stat_ in sets:
        for q in halves:
            put(upd_, q, update(mm3(chunk(tmp_, q), both(mat_)), q))
    for q in halves:
        v = mm3(chunk(cur, q), both(upd))
        roots_out[pl.ds(q * HALF, HALF)] = v
        put(mine, q, v)
        put(other, q, mm3(chunk(cur_b, q), both(upd_b)))
    v = split(grad_full[...].reshape(BS, BS))
    half = tuple(
        jnp.where(side_bit == 0, a, b) for a, b in zip(chunk(mine, 0), chunk(other, 1))
    )
    v = split(mm3(half, v))
    right = tuple(jnp.where(side_bit == 0, b, a) for a, b in zip(both(mine), both(other)))
    precond_out[...] = mm3(v, right)
    for copy in sends:
        copy.wait_send()


def shards(grad_out, acts, stat_old, root_old, assign):
    def wide(*shape):
        return pltpu.VMEM((*shape, UNIT, BS), jnp.int16)

    def narrow(*shape):
        return pltpu.VMEM((*shape, UNIT, HALF), jnp.int16)

    def steps(count, *shape):
        return pltpu.VMEM((*shape, 1, count), F32)

    def pair_of(rows_):
        return pltpu.VMEM((2, rows_, BS), BF)

    dma = pltpu.SemaphoreType.DMA
    anywhere = pl.BlockSpec(memory_space=pl.ANY)
    vmem = pl.BlockSpec(memory_space=pltpu.VMEM)
    roots, precond = pl.pallas_call(
        kernel,
        out_shape=(
            pltpu.VMEM((BS, BS), F32),
            pltpu.VMEM((HALF, BS), F32),
        ),
        in_specs=[pl.BlockSpec(memory_space=pltpu.SMEM), vmem, vmem, anywhere, anywhere],
        out_specs=(vmem, vmem),
        scratch_shapes=[
            pltpu.VMEM((CORES * Y, TOK, SHARD), BF),
            pltpu.VMEM((X, Z_LO, SUB, TOK), BF),
            pltpu.VMEM((BS, BS), F32),
            pltpu.VMEM((BS, BS), F32),
            pltpu.VMEM((Y, UNIT, HALF), F32),
            pltpu.VMEM((Z_LO, X, SUB, BS), F32),
            *[pair_of(BS) for _ in range(10)],
            pair_of(HALF),
            *[pair_of(BS) for _ in range(8)],
            pltpu.VMEM((BS, BS), F32),
            narrow(3, Y), narrow(3, Y), steps(HALF, 3, Y), steps(HALF, 3, Y),
            narrow(2, 2), narrow(2, 2), steps(HALF, 2, 2), steps(HALF, 2, 2),
            narrow(2, 2), narrow(3, 2), steps(HALF, 2, 2), steps(HALF, 3, 2),
            wide(2, 4), wide(2, 4),
            pltpu.VMEM((2, 4, 2, BS), F32), pltpu.VMEM((2, 4, 2, BS), F32),
            dma((3,)),
            dma((2, 4, 4)), dma((2, 4, 4)),
            dma((29,)), dma((29,)),
            dma((4, 3)), dma((4, 3)),
            dma((2, 3, Y)), dma((2, 3, Y)),
            dma((2, 2, 2)), dma((2, 2, 2)),
            dma((2, 3, 2)), dma((2, 3, 2)),
            dma((2, 2)), dma((2, 2)),
        ],
        compiler_params=pltpu.CompilerParams(
            collective_id=0, has_side_effects=True, vmem_limit_bytes=56 * 2**20
        ),
    )(assign, grad_out, acts, stat_old[0, 0], root_old[0, 0])
    return roots[None, None], precond[None, None]


def solution(mesh):
    placed = (
        P("tok", "blk"),
        P("tok", "blk"),
        P("tok", "blk", None, None),
        P("tok", "blk", None, None),
        P("blk", None),
    )
    return jax.shard_map(
        shards,
        mesh=mesh,
        in_specs=placed,
        out_specs=(P("tok", "blk", None, None), P("tok", "blk", None, None)),
        check_vma=False,
    )
```

```python
import math

import jax
import jax.numpy as jnp
from jax import lax
from jax.experimental import pallas as pl
from jax.experimental.pallas import tpu as pltpu
from jax.sharding import PartitionSpec as P

BETA = 0.9
DAMPING = 0.001
MESH = pl.DeviceIdType.MESH
BF = jnp.bfloat16
F32 = jnp.float32
X, Z_HI, Y, Z_LO, CORES = 4, 2, 8, 4, 2
BS = 512
HALF = 256
UNIT = 128
TOK = 1024
QT = 256
SUB = 32
OFFSETS = (0, 1, -1, 2, -2, 3, -3, 4)
TURNS = (2, 1, -1, 0)
RIGHTWARD = (0, 1, 3, 5)
STRAIGHT = 7
SHARD = 128
STEPS = 32767.0


def split(v):
    hi = v.astype(BF)
    lo = (v - hi.astype(F32)).astype(BF)
    return hi, lo


def dot(a, b):
    return jnp.dot(a, b, preferred_element_type=F32)


def dot_nt(a, b):
    return lax.dot_general(a, b, (((1,), (1,)), ((), ())), preferred_element_type=F32)


def mm3(a, b, d=dot):
    return d(a[0], b[0]) + (d(a[0], b[1]) + d(a[1], b[0]))


def encode(v):
    top = jnp.maximum(jnp.max(jnp.abs(v), axis=0, keepdims=True), 1e-30)
    code = jnp.round(v * (STEPS / top)).astype(jnp.int32).astype(jnp.int16)
    return code, top * (1.0 / STEPS)


def decode(code, step):
    return code.astype(jnp.int32).astype(F32) * step


def kernel(
    assign, grad, acts, stat_hbm, root_hbm, roots_out, precond_out,
    cols, rows, stat, root, hold, grad_full, ori, r2, r4, mat, upd, cur, upd2, tmp, mine, other, pre,
    ori_b, r4_b, mat_b, upd_b, cur_b, upd2_b, tmp_b, old_b, stat_b,
    xcs, xcr, xss, xsr, zcs, zcr, zss, zsr, acs, acr, ass_, asr, rcs, rcr, rss, rsr,
    loc_sem, ys, yr, sibs, sibr, ws, wr, xs, xr, zs, zr, as_, ar, rs, rr,
):
    t = lax.axis_index("tok")
    j = lax.axis_index("blk")
    x = lax.rem(t, X)
    h = lax.div(t, X)
    core = lax.rem(j, CORES)
    y = lax.rem(lax.div(j, CORES), Y)
    w = lax.div(j, CORES * Y)

    def y_dev(d):
        return (t, w * (CORES * Y) + lax.rem(y + d + Y, Y) * CORES + core)

    def w_dev(d):
        return (t, lax.rem(w + d + Z_LO, Z_LO) * (CORES * Y) + y * CORES + core)

    def x_dev(d):
        return (h * X + lax.rem(x + d + X, X), j)

    sibling = (t, j + 1 - 2 * core)
    z_dev = ((1 - h) * X + x, j)
    pair_dev = (t + 1 - 2 * lax.rem(x, 2), j)

    partners = [sibling, z_dev] + [y_dev(d) for d in (1, -1)]
    partners += [dev(d) for dev in (w_dev, x_dev) for d in (1, 2, 3)]

    stat_in = pltpu.make_async_copy(stat_hbm, stat, loc_sem.at[0])
    root_in = pltpu.make_async_copy(root_hbm, root, loc_sem.at[1])
    root_in.start()
    stat_in.start()

    barrier = pltpu.get_barrier_semaphore()
    for dev in partners:
        pl.semaphore_signal(barrier, inc=1, device_id=dev, device_id_type=MESH)
    pl.semaphore_wait(barrier, len(partners))

    sends = []

    def remote(src, dst, ssem, rsem, dev):
        return pltpu.make_async_remote_copy(
            src_ref=src, dst_ref=dst, send_sem=ssem, recv_sem=rsem, device_id=dev, device_id_type=MESH
        )

    def start(src, dst, ssem, rsem, dev):
        copy = remote(src, dst, ssem, rsem, dev)
        copy.start()
        sends.append(copy)

    def landed(dst, ssem, rsem, dev):
        remote(dst, dst, ssem, rsem, dev).wait_recv()

    def at_y(d):
        return lax.rem(y + d + Y, Y)

    SIDES = ((0, 1), (1, -1))

    def part(q):
        return pl.ds(q * QT, QT)

    def ring(d):
        return [((n + 2 * side) % 4, side, step) for n in range(4 if d < 4 else 2) for side, step in SIDES]

    def number(d, q, side):
        return 24 + q if d == 4 else ((d - 1) * 4 + q) * 2 + side

    def y_step(d, parts):
        for q, side, step in ring(d):
            if (q + 2 * side) % 4 not in parts:
                continue
            region = cols.at[at_y(-step * d) * CORES + core, part(q)]
            landed(region, ys.at[side, d - 1, q], yr.at[side, d - 1, q], y_dev(-step))
            if d < 3 or (d == 3 and q // 2 == side):
                start(region, region, ys.at[side, d, q], yr.at[side, d, q], y_dev(step))
            n = number(d, q, side)
            start(region, region, sibs.at[n], sibr.at[n], sibling)

    def y_ready(d):
        if d == 0:
            own_in.wait()
            landed(cols.at[y * CORES + 1 - core], sibs.at[28], sibr.at[28], sibling)
            return
        for q, side, step in ring(d):
            n = number(d, q, side)
            landed(cols.at[at_y(-step * d) * CORES + 1 - core, part(q)], sibs.at[n], sibr.at[n], sibling)

    def quarter(e):
        return lax.rem(x + TURNS[e] + X, X)

    def rows_ready(e):
        for d in (2, 3, 1):
            unit = rows.at[quarter(e), lax.rem(w - d + Z_LO, Z_LO)]
            landed(unit, ws.at[e, d - 1], wr.at[e, d - 1], w_dev(-d))

    for q, side, step in ring(0):
        start(acts.at[part(q)], cols.at[y * CORES + core, part(q)], ys.at[side, 0, q], yr.at[side, 0, q], y_dev(step))
    start(acts, cols.at[y * CORES + core], sibs.at[28], sibr.at[28], sibling)
    own_in = pltpu.make_async_copy(acts, cols.at[y * CORES + core], loc_sem.at[2])
    own_in.start()
    v = grad[...].T
    for q in range(4):
        rows[q, w] = v[q * SUB:(q + 1) * SUB]

    def rows_send(e):
        unit = rows.at[quarter(e), w]
        for d in (2, 3, 1):
            start(unit, unit, ws.at[e, d - 1], wr.at[e, d - 1], w_dev(d))

    rows_send(0)
    def eye(low_row, count):
        r = lax.broadcasted_iota(jnp.int32, (count, BS), 0) + low_row
        c = lax.broadcasted_iota(jnp.int32, (count, BS), 1)
        return r == c

    def old_send(n, ref):
        for u in range(4):
            value = ref[pl.ds(u * UNIT, UNIT)]
            on = eye(u * UNIT, UNIT)
            code, step = encode(jnp.where(on, 0.0, value))
            rcs[n, u] = code
            rss[n, u, 0:1] = step
            rss[n, u, 1:2] = jnp.sum(jnp.where(on, value, 0.0), axis=0, keepdims=True)
        start(rcs.at[n], rcr.at[n], rs.at[0, n], rr.at[0, n], pair_dev)
        start(rss.at[n], rsr.at[n], rs.at[1, n], rr.at[1, n], pair_dev)

    def old_landed(n):
        landed(rcr.at[n], rs.at[0, n], rr.at[0, n], pair_dev)
        landed(rsr.at[n], rs.at[1, n], rr.at[1, n], pair_dev)

    def old_take(n, u):
        return decode(rcr[n, u], rsr[n, u, 0:1]) + jnp.where(eye(u * UNIT, UNIT), rsr[n, u, 1:2], 0.0)

    root_in.wait()
    old_send(0, root)
    x0 = split(root[...])
    mine[0] = x0[0]
    mine[1] = x0[1]

    scaling = 1.0 / math.sqrt(TOK * X * Z_HI)

    def piece(e, g):
        left = rows[quarter(e)].reshape(UNIT, TOK)
        at = at_y(OFFSETS[g]) * CORES
        right = jnp.concatenate([cols[at], cols[at + 1]], axis=1)
        return dot(left, right) * scaling

    RIGHT, LEFT, FAR = 0, 1, 2

    def heading(slot, g):
        if slot == FAR:
            return 2 if g == STRAIGHT else (1 if g in RIGHTWARD else -1)
        return 1 if slot == RIGHT else -1

    def x_send(slot, g, value):
        code, step = encode(value)
        xcs[slot, g] = code
        xss[slot, g] = step
        dev = x_dev(heading(slot, g))
        start(xcs.at[slot, g], xcr.at[slot, g], xs.at[0, slot, g], xr.at[0, slot, g], dev)
        start(xss.at[slot, g], xsr.at[slot, g], xs.at[1, slot, g], xr.at[1, slot, g], dev)

    def x_take(slot, g):
        dev = x_dev(-heading(slot, g))
        landed(xcr.at[slot, g], xs.at[0, slot, g], xr.at[0, slot, g], dev)
        landed(xsr.at[slot, g], xs.at[1, slot, g], xr.at[1, slot, g], dev)
        return decode(xcr[slot, g], xsr[slot, g])

    def far(*gs):
        for g in gs:
            x_send(FAR, g, piece(0, g))

    def raw(slot, *gs):
        for g in gs:
            x_send(slot, g, piece(slot + 1, g))

    def add(slot, *gs):
        for g in gs:
            x_send(slot, g, piece(slot + 1, g) + x_take(FAR, g))

    y_step(1, (0, 1))
    rows_send(1)
    y_step(1, (2, 3))
    y_ready(0)
    y_ready(1)
    rows_ready(0)
    far(0, 2, 1)
    y_step(2, (0, 1))
    rows_send(2)
    y_step(2, (2, 3))
    y_ready(2)
    far(3, 4)
    rows_ready(1)
    rows_send(3)
    raw(RIGHT, 2)
    add(RIGHT, 0)
    y_step(3, (0, 1))
    raw(RIGHT, 4)
    add(RIGHT, 1)
    y_step(3, (2, 3))
    rows_ready(2)
    raw(LEFT, 0, 1)
    add(LEFT, 2)
    y_ready(3)
    far(5, 6)
    raw(LEFT, 3)
    add(LEFT, 4)
    y_step(4, (0, 1))
    add(RIGHT, 3)
    raw(RIGHT, 6)
    raw(LEFT, 5)
    add(RIGHT, 5)
    add(LEFT, 6)
    y_ready(4)
    far(7)
    raw(LEFT, 7)
    raw(RIGHT, 7)
    stat_in.wait()
    old_send(1, stat)
    rows_ready(3)
    for g in range(8):
        hold[at_y(OFFSETS[g])] = piece(3, g)

    for g in range(8):
        where = at_y(OFFSETS[g])
        v = hold[where] + x_take(RIGHT, g) + x_take(LEFT, g)
        hold[where] = v + x_take(FAR, g) if g == STRAIGHT else v

    mine_pair = lax.div(x, 2)

    def block(to_h, i, c):
        pair = to_h * 2 + (1 - mine_pair if i == 0 else mine_pair)
        return hold[2 * lax.div(assign[0, 2 * pair], 2) + c]

    UNITS = [(i, c) for i in range(2) for c in range(2)]
    for i, c in UNITS:
        code, step = encode(block(1 - h, i, c))
        zcs[i, c] = code
        zss[i, c] = step
        start(zcs.at[i, c], zcr.at[i, c], zs.at[0, i, c], zr.at[0, i, c], z_dev)
        start(zss.at[i, c], zsr.at[i, c], zs.at[1, i, c], zr.at[1, i, c], z_dev)

    old_landed(0)
    for u in range(4):
        v = split(old_take(0, u))
        old_b[0, pl.ds(u * UNIT, UNIT)] = v[0]
        old_b[1, pl.ds(u * UNIT, UNIT)] = v[1]
    v = (old_b[0], old_b[1])
    v = split(mm3(v, v))
    v = split(mm3(v, v))
    r4_b[0] = v[0]
    r4_b[1] = v[1]

    v = split(mm3((mine[0], mine[1]), (mine[0], mine[1])))
    r2[0] = v[0]
    r2[1] = v[1]
    v = split(mm3(v, v))
    r4[0] = v[0]
    r4[1] = v[1]

    near = 1 - 2 * lax.rem(x, 2)
    across = [(0, near, 1), (1, 2, 0), (2, -near, 0)]

    def place(where, c, value):
        for q in range(4):
            grad_full[q, where, :, c * HALF:(c + 1) * HALF] = value[q * SUB:(q + 1) * SUB]

    for i, c in UNITS:
        landed(zcr.at[i, c], zs.at[0, i, c], zr.at[0, i, c], z_dev)
        landed(zsr.at[i, c], zs.at[1, i, c], zr.at[1, i, c], z_dev)
        v = block(h, i, c) + decode(zcr[i, c], zsr[i, c])
        code, step = encode(v)
        acs[i, c] = code
        ass_[i, c] = step
        for n, d, unit in across:
            if unit == i:
                start(acs.at[i, c], acr.at[n, c], as_.at[0, n, c], ar.at[0, n, c], x_dev(d))
                start(ass_.at[i, c], asr.at[n, c], as_.at[1, n, c], ar.at[1, n, c], x_dev(d))
        if i == 1:
            place(x, c, v)
    old_landed(1)
    for u in range(4):
        stat_b[pl.ds(u * UNIT, UNIT)] = old_take(1, u)
    for n, d, unit in (across[1], across[2], across[0]):
        for c in range(2):
            landed(acr.at[n, c], as_.at[0, n, c], ar.at[0, n, c], x_dev(d))
            landed(asr.at[n, c], as_.at[1, n, c], ar.at[1, n, c], x_dev(d))
            place(lax.rem(x + d + X, X), c, decode(acr[n, c], asr[n, c]))

    side_bit = lax.rem(assign[0, t], 2)
    g = grad_full[...].reshape(BS, BS)
    gt = g.T
    for ref, value in ((ori, jnp.where(side_bit == 0, g, gt)), (ori_b, jnp.where(side_bit == 0, gt, g))):
        v = split(value)
        ref[0] = v[0]
        ref[1] = v[1]

    def both(ref):
        return ref[0], ref[1]

    def chunk(ref, q):
        return ref[0, pl.ds(q * HALF, HALF)], ref[1, pl.ds(q * HALF, HALF)]

    def put(ref, q, value):
        value = split(value)
        ref[0, pl.ds(q * HALF, HALF)] = value[0]
        ref[1, pl.ds(q * HALF, HALF)] = value[1]

    def update(value, q):
        return (jnp.where(eye(q * HALF, HALF), 5.0, 0.0) - value) * 0.25

    tokens = float(TOK * X * Z_HI)
    own_set = (ori, r4, mat, upd, cur, upd2, tmp, mine, stat)
    other_set = (ori_b, r4_b, mat_b, upd_b, cur_b, upd2_b, tmp_b, old_b, stat_b)
    sets = (own_set, other_set)
    halves = range(2)
    for ori_, r4_, mat_, upd_, cur_, upd2_, tmp_, old_, stat_ in sets:
        for q in halves:
            square = mm3(chunk(ori_, q), both(ori_), dot_nt) * (1.0 / tokens)
            damp = jnp.where(eye(q * HALF, HALF), DAMPING, 0.0)
            put(tmp_, q, BETA * stat_[pl.ds(q * HALF, HALF)] + (1.0 - BETA) * square + damp)
    for ori_, r4_, mat_, upd_, cur_, upd2_, tmp_, old_, stat_ in sets:
        for q in halves:
            v = mm3(chunk(r4_, q), both(tmp_))
            put(mat_, q, v)
            put(upd_, q, update(v, q))
    for ori_, r4_, mat_, upd_, cur_, upd2_, tmp_, old_, stat_ in sets:
        for q in halves:
            put(upd2_, q, mm3(chunk(upd_, q), both(upd_)))
        for q in halves:
            put(cur_, q, mm3(chunk(old_, q), both(upd_)))
    for ori_, r4_, mat_, upd_, cur_, upd2_, tmp_, old_, stat_ in sets:
        for q in halves:
            put(tmp_, q, mm3(chunk(upd2_, q), both(upd2_)))
    for ori_, r4_, mat_, upd_, cur_, upd2_, tmp_, old_, stat_ in sets:
        for q in halves:
            put(upd_, q, update(mm3(chunk(tmp_, q), both(mat_)), q))
    for q in halves:
        v = mm3(chunk(cur, q), both(upd))
        roots_out[pl.ds(q * HALF, HALF)] = v
        put(mine, q, v)
        put(other, q, mm3(chunk(cur_b, q), both(upd_b)))
    v = split(grad_full[...].reshape(BS, BS))
    half = tuple(
        jnp.where(side_bit == 0, a, b) for a, b in zip(chunk(mine, 0), chunk(other, 1))
    )
    v = split(mm3(half, v))
    right = tuple(jnp.where(side_bit == 0, b, a) for a, b in zip(both(mine), both(other)))
    precond_out[...] = mm3(v, right)
    for copy in sends:
        copy.wait_send()


def shards(grad_out, acts, stat_old, root_old, assign):
    def wide(*shape):
        return pltpu.VMEM((*shape, UNIT, BS), jnp.int16)

    def narrow(*shape):
        return pltpu.VMEM((*shape, UNIT, HALF), jnp.int16)

    def steps(count, *shape):
        return pltpu.VMEM((*shape, 1, count), F32)

    def pair_of(rows_):
        return pltpu.VMEM((2, rows_, BS), BF)

    dma = pltpu.SemaphoreType.DMA
    anywhere = pl.BlockSpec(memory_space=pl.ANY)
    vmem = pl.BlockSpec(memory_space=pltpu.VMEM)
    roots, precond = pl.pallas_call(
        kernel,
        out_shape=(
            pltpu.VMEM((BS, BS), F32),
            pltpu.VMEM((HALF, BS), F32),
        ),
        in_specs=[pl.BlockSpec(memory_space=pltpu.SMEM), vmem, vmem, anywhere, anywhere],
        out_specs=(vmem, vmem),
        scratch_shapes=[
            pltpu.VMEM((CORES * Y, TOK, SHARD), BF),
            pltpu.VMEM((X, Z_LO, SUB, TOK), BF),
            pltpu.VMEM((BS, BS), F32),
            pltpu.VMEM((BS, BS), F32),
            pltpu.VMEM((Y, UNIT, HALF), F32),
            pltpu.VMEM((Z_LO, X, SUB, BS), F32),
            *[pair_of(BS) for _ in range(10)],
            pair_of(HALF),
            *[pair_of(BS) for _ in range(8)],
            pltpu.VMEM((BS, BS), F32),
            narrow(3, Y), narrow(3, Y), steps(HALF, 3, Y), steps(HALF, 3, Y),
            narrow(2, 2), narrow(2, 2), steps(HALF, 2, 2), steps(HALF, 2, 2),
            narrow(2, 2), narrow(3, 2), steps(HALF, 2, 2), steps(HALF, 3, 2),
            wide(2, 4), wide(2, 4),
            pltpu.VMEM((2, 4, 2, BS), F32), pltpu.VMEM((2, 4, 2, BS), F32),
            dma((3,)),
            dma((2, 4, 4)), dma((2, 4, 4)),
            dma((29,)), dma((29,)),
            dma((4, 3)), dma((4, 3)),
            dma((2, 3, Y)), dma((2, 3, Y)),
            dma((2, 2, 2)), dma((2, 2, 2)),
            dma((2, 3, 2)), dma((2, 3, 2)),
            dma((2, 2)), dma((2, 2)),
        ],
        compiler_params=pltpu.CompilerParams(
            collective_id=0, has_side_effects=True, vmem_limit_bytes=56 * 2**20
        ),
    )(assign, grad_out, acts, stat_old[0, 0], root_old[0, 0])
    return roots[None, None], precond[None, None]


def solution(mesh):
    placed = (
        P("tok", "blk"),
        P("tok", "blk"),
        P("tok", "blk", None, None),
        P("tok", "blk", None, None),
        P("blk", None),
    )
    return jax.shard_map(
        shards,
        mesh=mesh,
        in_specs=placed,
        out_specs=(P("tok", "blk", None, None), P("tok", "blk", None, None)),
        check_vma=False,
    )
```
